512 devices in a mesh: scen: 16 (over x, y), comp: 32 (over z, core).
Axes of the slice: x: 4, y: 4, z: 16, core: 2. Of those that a mesh axis runs over, the one named last changes fastest.
Arguments:
- multiplier: float32 [256, 52, 16384], P('scen', None, 'comp'), may hold values from -2 to 2
- consensus_old: float32 [16, 52, 16384], P(None, None, 'comp'), may hold values from 0 to 1
- failure_week: int32 [256, 16384], P('scen', 'comp'), may hold values from 0 to 51
- crew_index: int32 [16384], P('comp'), may hold values from 0 to 255
- labor_hours: float32 [16384], P('comp'), may hold values from 0.5 to 1.5
- capacity: float32 [256, 52], replicated, may hold values from 6 to 25
- risk_weight: float32 [16384], P('comp'), may hold values from 0.5 to 2
- likelihood: float32 [256], P('scen'), may hold values from 0.1 to 1
- bundle_index: int32 [256], P('scen'), may hold values from 0 to 15, never falling along the last dimension, each value on 1 to 32 neighbouring positions
Outputs:
- multiplier_new: float32 [256, 52, 16384], P('scen', None, 'comp')
- bundle_consensus: float32 [256, 52, 16384], P('scen', None, 'comp')
The draws below stay inside these ranges and needn't reach their ends.
Inputs may be any that keep to these rules, and one draw needn't show every extreme that they name: `bundle_index`: never falls along the scenarios; every bundle holds 1 to 32 scenarios, one exactly 32.
All inputs are finite; a program needn't handle non-finite values.
Results may differ from the reference program's by a relative error of at most 0.00013.
Values sent between devices are 32-bit elements; how exact they have to be, the bound alone decides.
A program may use at most 64 MiB of HBM per device.

```python
import math
import jax
import jax.numpy as jnp
import numpy as np

W = 52
S_DEV = 16
CREWS = 256
ITERS = 3
SCEN = 256
NC = 16384
NB = 16


def plant(result, stream_key, least, high):
    index_at = [jax.random.randint(jax.random.fold_in(stream_key, axis), (), 0, length) for axis, length in enumerate(result.shape)]
    longest = result.shape.index(max(result.shape))
    beside = index_at[:longest] + [(index_at[longest] + 1) % result.shape[longest]] + index_at[longest + 1:]
    return result.at[tuple(index_at)].set(least).at[tuple(beside)].set(high)


def levels(own_key, dims, pieces, smallest, high):
    factor_of, own = 1.0, jax.random.fold_in(own_key, 6)
    for axis_at, blocks in pieces:
        steps = jnp.exp(jax.random.uniform(jax.random.fold_in(own, axis_at), (blocks,), jnp.float32, smallest / len(pieces), high / len(pieces)))
        factor_of = factor_of * jnp.repeat(steps, dims[axis_at] // blocks).reshape([-1 if axis == axis_at else 1 for axis in range(len(dims))])
    return factor_of


def profile(number_of, total, limit, skew):
    weights = [(1 << 20) // math.isqrt(standing ** skew) + 1 for standing in range(2, number_of + 1)]
    surplus, counts = total - limit - (number_of - 1), [1] * (number_of - 1)
    while surplus > 0:
        movable = [i for i in range(number_of - 1) if counts[i] < limit]
        mass, budget = sum([weights[i] for i in movable]), surplus
        for i in movable:
            addition = min(limit - counts[i], max(1, budget * weights[i] // mass), surplus)
            counts[i] = counts[i] + addition
            surplus = surplus - addition
    return np.array([limit] + counts)


def ragged_sizes(key, amount, total, reach, skew):
    if amount == 2:
        one = jax.random.randint(key, (), max(1, total - reach), min(reach, total - 1) + 1)
        return jnp.stack([one, total - one])
    tallies = jnp.asarray(profile(amount, total, reach, skew), jnp.int32)
    couples = (amount - 1) // 2
    source_of, taker = tallies[1:1 + 2 * couples:2], tallies[2:2 + 2 * couples:2]
    room = jnp.minimum(source_of - 1, reach - taker)
    moved = jax.random.randint(jax.random.fold_in(key, 1), (couples,), 0, 1 << 20) % (room + 1)
    tallies = tallies.at[1:1 + 2 * couples:2].set(source_of - moved).at[2:2 + 2 * couples:2].set(taker + moved)
    return tallies[jax.random.permutation(jax.random.fold_in(key, 2), amount)]


def scatter_about(rng, shape, deviation, reach, pieces=(), held_as=jnp.bfloat16):
    loudness = levels(rng, shape, pieces, -0.22, 0.18) if pieces else 1.0
    values = jax.random.normal(rng, shape, jnp.float32) * deviation * loudness
    return jnp.minimum(jnp.maximum(values, -reach), reach).astype(held_as)


def setup_inputs(seed: int = 0) -> dict:
    splits = jax.random.split(jax.random.key(seed), 10)
    return {
        "multiplier": scatter_about(splits[0], (SCEN, W, NC), 0.3, 2.0, ((0, 16), (2, 32)), jnp.float32),
        "consensus_old": jnp.clip(1.0 * jax.random.uniform(splits[1], (NB, W, NC), jnp.float32) ** levels(splits[1], (NB, W, NC), ((2, 32),), -0.2, 0.2), 0.0, 1.0),
        "failure_week": plant(jax.random.randint(splits[2], (SCEN, NC), 0, W), jax.random.fold_in(splits[2], 1), 0, W - 1).astype(jnp.int32),
        "crew_index": plant(jax.random.randint(splits[3], (NC,), 0, CREWS), jax.random.fold_in(splits[3], 1), 0, CREWS - 1).astype(jnp.int32),
        "labor_hours": jnp.clip(jnp.exp(math.log(1.5) - 1.0986123 * jax.random.uniform(splits[4], (NC,), jnp.float32) ** levels(splits[4], (NC,), ((0, 32),), -0.2, 0.2)), 0.5, 1.5),
        "capacity": jnp.clip(jax.random.uniform(splits[5], (CREWS, W), jnp.float32, 6.0, 25.0), 6.0, 25.0),
        "risk_weight": jnp.clip(jnp.exp(math.log(2.0) - 1.3862944 * jax.random.uniform(splits[6], (NC,), jnp.float32) ** levels(splits[6], (NC,), ((0, 32),), -0.2, 0.2)), 0.5, 2.0),
        "likelihood": jnp.clip(jnp.exp(math.log(1.0) - 2.3025851 * jax.random.uniform(splits[7], (SCEN,), jnp.float32) ** levels(splits[7], (SCEN,), ((0, 16),), -0.2, 0.2)), 0.1, 1.0),
        "bundle_index": jnp.searchsorted(jnp.cumsum(ragged_sizes(splits[8], NB, SCEN, 2 * S_DEV, 2)), jnp.arange(SCEN), side="right").astype(jnp.int32),
    }


step_size = 0.18
penalty = 1.0
crew_weight = 1.0


def target_plan(failure_week, week_count):
    week_index = jnp.arange(week_count, dtype=jnp.int32)[None, :, None]
    spacing = (failure_week[:, None, :] - week_index).astype(jnp.float32)
    return jnp.where(spacing >= 0, 1.0 / (1.0 + (spacing / 4.0) ** 2), 0.25).astype(jnp.float32)


def reference(multiplier, consensus_old, failure_week, crew_index, labor_hours, capacity, risk_weight, likelihood, bundle_index):
    anchor = jnp.take(consensus_old, bundle_index, axis=0)
    target = target_plan(failure_week, W)
    coupling = crew_weight * CREWS / NC
    plan = anchor
    for sweep in range(ITERS):
        crew_load = jax.ops.segment_sum(jnp.moveaxis(plan * labor_hours, 2, 0), crew_index, CREWS)
        excess = jnp.maximum(crew_load - capacity[:, None, :], 0.0)
        pushed = jnp.moveaxis(jnp.take(excess, crew_index, axis=0), 0, 2)
        slope = risk_weight * (plan - target) + multiplier + penalty * (plan - anchor) + coupling * labor_hours * pushed
        plan = jnp.clip(plan - step_size * slope, 0.0, 1.0)
    weight_sum = jax.ops.segment_sum(likelihood, bundle_index, NB)
    totals = jax.ops.segment_sum(likelihood[:, None, None] * plan, bundle_index, NB)
    consensus = totals / weight_sum[:, None, None]
    bundle_consensus = jnp.take(consensus, bundle_index, axis=0)
    multiplier_new = multiplier + penalty * (plan - bundle_consensus)
    return multiplier_new, bundle_consensus
```

```python
import jax
import jax.numpy as jnp
from jax import lax
from jax.experimental import pallas as pl
from jax.experimental.pallas import tpu as pltpu
from jax.sharding import PartitionSpec as P

MESH = pl.DeviceIdType.MESH
ITERS = 3
STEP = 0.18
CREW_WEIGHT = 1.0
PLACES = (6, -6, 3, -3, 0, 7, -5, 4, -2, 1, 5, -7, 2, -4, -1, 8)
GROUPS = ((0, 24), (24, 32))
NCOPY = 17


def split(x):
    high = x.astype(jnp.bfloat16)
    low = (x - high.astype(jnp.float32)).astype(jnp.bfloat16)
    return high, low


def kernel(
    mult_hbm, cons_hbm, fw_ref, crew_ref, labor_ref, cap_ref, risk_ref, like_ref, bundle_ref,
    new_ref, bc_ref,
    mult, cons, plan, base, hot, cap_t, cap_pad, runs, sums,
    part0, part1, core0, core1, near0, near1, opp0, opp1, hub0, hub1, far0, far1, exc0, exc1,
    edge0, edge1, got0, got1,
    load_sem, send_sem, recv_sem, edge_send, edge_recv,
):
    scen_count = lax.axis_size("scen")
    comp_count = lax.axis_size("comp")
    chips = comp_count // 2
    me_s = lax.axis_index("scen")
    me_c = lax.axis_index("comp")
    z = me_c // 2
    k = lax.rem(me_c, 2)
    rows_s, weeks, cols = mult.shape
    crews = hot.shape[0]
    half = crews // 2
    parts, cores, nears, opps = (part0, part1), (core0, core1), (near0, near1), (opp0, opp1)
    hubs, fars, excs = (hub0, hub1), (far0, far1), (exc0, exc1)
    edges, gots = (edge0, edge1), (got0, got1)

    def chip(step):
        return (me_s, lax.rem(z + step + chips, chips) * 2 + k)

    def row(step):
        return (lax.rem(me_s + step + scen_count, scen_count), me_c)

    other = (me_s, z * 2 + 1 - k)

    cons_in = pltpu.make_async_copy(cons_hbm, cons, load_sem.at[0])
    mult_in = pltpu.make_async_copy(mult_hbm, mult, load_sem.at[1])
    cons_in.start()
    mult_in.start()

    barrier = pltpu.get_barrier_semaphore()
    greeted = [other] + [chip(n) for n in (1, -1, 2, -2, 3, -3, 6, -6)] + [row(1), row(-1)]
    for device in greeted:
        pl.semaphore_signal(barrier, inc=1, device_id=device, device_id_type=MESH)

    hot[...] = (
        lax.broadcasted_iota(jnp.int32, (crews, cols), 0) == crew_ref[...]
    ).astype(jnp.bfloat16)
    cap_pad[...] = jnp.zeros_like(cap_pad)
    cap_pad[:, :weeks] = cap_ref[pl.ds(pl.multiple_of(k * half, half), half), :]
    cap_t[...] = cap_pad[...].T
    plan[...] = jnp.zeros_like(plan)
    base[...] = jnp.zeros_like(base)
    labor = labor_ref[...]
    risk = risk_ref[...]
    coupling = CREW_WEIGHT * crews / (cols * comp_count)
    alpha = 1.0 - STEP * (risk + 1.0)
    beta = (STEP * coupling) * labor

    def scenario(place):
        return lax.rem(z + PLACES[place] + chips, chips)

    def load(g, place, x):
        rows = GROUPS[g][1]
        high, low = split(x * labor)
        dims = (((1,), (1,)), ((), ()))
        out = lax.dot_general(high, hot[...], dims, preferred_element_type=jnp.float32)
        out = out + lax.dot_general(low, hot[...], dims, preferred_element_type=jnp.float32)
        count = x.shape[0] // rows
        for h in range(2):
            parts[g][h, pl.ds(place, count)] = out[:, h * half:(h + 1) * half].reshape(
                count, rows, half
            )

    def copy(g, t, n, source, target, device):
        at = (g * ITERS + t) * NCOPY + n
        return pltpu.make_async_remote_copy(
            src_ref=source, dst_ref=target, send_sem=send_sem.at[at], recv_sem=recv_sem.at[at],
            device_id=device, device_id_type=MESH,
        )

    flying = {}

    def sent(g, t, numbers):
        for n in numbers:
            flying.pop((g, t, n)).wait_send()

    def arrive(g, t, numbers):
        for n in numbers:
            flying[g, t, n].wait_recv()

    def start(g, t, n, source, target, device):
        c = copy(g, t, n, source, target, device)
        c.start()
        flying[g, t, n] = c

    def update(g, t):
        first, rows = GROUPS[g]
        for place in range(0, rows_s, 4):
            scens = pl.ds(place, 4)
            weeks_at = pl.ds(first, rows)
            old = plan[scens, weeks_at, :].reshape(4 * rows, cols)
            if t >= 0:
                pushed = 0.0
                for h in range(2):
                    high, low = split(excs[g][t, h, scens].reshape(4 * rows, half))
                    way = hot[h * half:(h + 1) * half, :]
                    pushed = pushed + jnp.dot(high, way, preferred_element_type=jnp.float32)
                    pushed = pushed + jnp.dot(low, way, preferred_element_type=jnp.float32)
                old = jnp.clip(
                    alpha * old + base[scens, weeks_at, :].reshape(4 * rows, cols) - beta * pushed,
                    0.0, 1.0,
                )
                if t < ITERS - 1:
                    plan[scens, weeks_at, :] = old.reshape(4, rows, cols)
                else:
                    for n in range(4):
                        runs[scenario(place + n), weeks_at, :] = old[n * rows:(n + 1) * rows]
            if t < ITERS - 1:
                load(g, place, old)

    def phase_core(g, t):
        if t > 0:
            sent(g, t - 1, (0,))
        update(g, t - 1)
        if t == 0 and g == 0:
            pl.semaphore_wait(barrier, len(greeted))
        start(g, t, 0, parts[g].at[1 - k], cores[g].at[t], other)

    def phase_near(g, t):
        arrive(g, t, (0,))
        cores[g][t] = cores[g][t] + parts[g][k]
        mine = cores[g].at[t]
        start(g, t, 1, mine.at[pl.ds(5, 5)], nears[g].at[t, 0], chip(1))
        start(g, t, 2, mine.at[pl.ds(10, 5)], nears[g].at[t, 1], chip(-1))
        start(g, t, 3, mine.at[15], opps[g].at[t], chip(4 * k - 2))

    def phase_far(g, t):
        if t > 0:
            sent(g, t - 1, (4, 5, 6, 7))
        arrive(g, t, (1, 2, 3))
        hubs[g][...] = cores[g][t, 0:5] + nears[g][t, 0] + nears[g][t, 1]
        hubs[g][1 - k] = hubs[g][1 - k] + opps[g][t]
        for n, step in enumerate((6, -6, 3, -3)):
            start(g, t, 4 + n, hubs[g].at[n], fars[g].at[t, n], chip(step))

    def phase_back(g, t):
        arrive(g, t, range(4, 8))
        far = fars[g][t]
        total = hubs[g][4] + (far[0] + far[1]) + (far[2] + far[3])
        first, rows = GROUPS[g]
        excs[g][t, k, 4] = jnp.maximum(total - cap_t[first:first + rows, :], 0.0)
        own = excs[g].at[t, k, 4]
        for n, step in enumerate((6, -6, 3, -3)):
            start(g, t, 8 + n, own, excs[g].at[t, k, n ^ 1], chip(step))

    def phase_spread(g, t):
        arrive(g, t, range(8, 12))
        mine = excs[g].at[t, k]
        start(g, t, 12, mine.at[pl.ds(0, 5)], mine.at[pl.ds(10, 5)], chip(1))
        start(g, t, 13, mine.at[pl.ds(0, 5)], mine.at[pl.ds(5, 5)], chip(-1))
        start(g, t, 14, mine.at[1 - k], mine.at[15], chip(2 - 4 * k))
        start(g, t, 15, mine.at[pl.ds(0, 5)], mine.at[pl.ds(0, 5)], other)

    def phase_share(g, t):
        arrive(g, t, (12, 13, 14))
        mine = excs[g].at[t, k]
        start(g, t, 16, mine.at[pl.ds(5, 11)], mine.at[pl.ds(5, 11)], other)

    def phase_end(g, t):
        arrive(g, t, (15, 16))

    cons_in.wait()
    for place in range(rows_s):
        plan[place, :weeks, :] = cons[bundle_ref[scenario(place)]]
    groups = range(len(GROUPS))
    for t in range(ITERS):
        for g in groups:
            if t > 0:
                phase_end(g, t - 1)
            phase_core(g, t)
        for g in groups:
            phase_near(g, t)
        if t == 0:
            mult_in.wait()
            week = lax.broadcasted_iota(jnp.int32, (weeks, cols), 0)
            for place in range(rows_s):
                d = scenario(place)
                spacing = (fw_ref[pl.ds(d, 1), :] - week).astype(jnp.float32)
                target = jnp.where(spacing >= 0, 1.0 / (1.0 + (spacing * 0.25) ** 2), 0.25)
                base[place, :weeks, :] = STEP * (
                    risk * target - mult[d] + plan[place, :weeks, :]
                )
        for phase in (phase_far, phase_back, phase_spread, phase_share):
            for g in groups:
                phase(g, t)

    last = rows_s - 1
    head, tail = bundle_ref[0], bundle_ref[last]
    moving = {}

    def edge_start(g, n, source, step):
        at = g * 4 + n
        moving[g, n] = pltpu.make_async_remote_copy(
            src_ref=source, dst_ref=gots[g].at[n], send_sem=edge_send.at[at],
            recv_sem=edge_recv.at[at], device_id=row(step), device_id_type=MESH,
        )
        moving[g, n].start()

    for g in groups:
        first, rows = GROUPS[g]
        phase_end(g, ITERS - 1)
        update(g, ITERS - 1)
        for n, (which, step) in enumerate(((tail, 1), (head, -1))):

            def body(s, carry):
                total, weight = carry
                factor = jnp.where(bundle_ref[s] == which, like_ref[s], 0.0)
                return total + factor * runs[s, first:first + rows, :], weight + factor

            total, weight = lax.fori_loop(
                0, rows_s, body, (jnp.zeros((rows, cols), jnp.float32), jnp.float32(0.0))
            )
            edges[g][n, 0:rows] = total
            edges[g][n, rows:rows + 8] = jnp.where(
                lax.broadcasted_iota(jnp.int32, (8, cols), 0) < 4,
                which.astype(jnp.float32), weight,
            )
            edge_start(g, n, edges[g].at[n], step)
    for g in groups:
        for n, step in enumerate((1, -1)):
            moving[g, n].wait_recv()
            edge_start(g, n + 2, gots[g].at[n], step)
    for g in groups:
        first, rows = GROUPS[g]
        live = min(weeks - first, rows)
        got = gots[g]
        for n in (2, 3):
            moving[g, n].wait_recv()

        def arrived(n, which):
            same = got[n, rows:rows + 1, :] == which.astype(jnp.float32)
            return (
                jnp.where(same, got[n, 0:rows], 0.0),
                jnp.where(same, got[n, rows + 4:rows + 5, :], 0.0),
            )

        def both(n, which):
            one, two = arrived(n, which), arrived(n + 2, which)
            return one[0] + two[0], one[1] + two[1]

        total, weight = both(0, head)
        for s in range(rows_s):
            if s:
                keep = jnp.where(bundle_ref[s] == bundle_ref[s - 1], 1.0, 0.0)
                total, weight = total * keep, weight * keep
            total = total + like_ref[s] * runs[s, first:first + rows, :]
            weight = weight + like_ref[s]
            if s < last:
                sums[s, 0:rows] = total
                sums[s, rows:rows + 1] = weight
        add = both(1, tail)
        mean = (total + add[0]) / (weight + add[1])
        for s in range(last, -1, -1):
            if s < last:
                mean = jnp.where(
                    bundle_ref[s] == bundle_ref[s + 1],
                    mean, sums[s, 0:rows] / sums[s, rows:rows + 1],
                )
            weeks_at = slice(first, first + live)
            bc_ref[s, weeks_at, :] = mean[:live]
            new_ref[s, weeks_at, :] = (
                mult[s, weeks_at, :] + (runs[s, weeks_at, :] - mean[:live])
            )
    for c in (*flying.values(), *moving.values()):
        c.wait_send()


def local(
    multiplier, consensus_old, failure_week, crew_index, labor_hours, capacity, risk_weight,
    likelihood, bundle_index,
):
    rows_s, weeks, cols = multiplier.shape
    crews = capacity.shape[0]
    half = crews // 2
    padded = sum(rows for _, rows in GROUPS)
    f32 = jnp.float32

    def each(*shape):
        return [
            pltpu.VMEM(tuple(rows + 8 if n == "e" else rows if n == "r" else n for n in shape), f32)
            for _, rows in GROUPS
        ]

    vmem, smem, anywhere = (
        pl.BlockSpec(memory_space=m) for m in (pltpu.VMEM, pltpu.SMEM, pl.ANY)
    )
    copies = len(GROUPS) * ITERS * NCOPY
    return pl.pallas_call(
        kernel,
        out_shape=[jax.ShapeDtypeStruct(multiplier.shape, f32)] * 2,
        in_specs=[anywhere, anywhere, vmem, vmem, vmem, vmem, vmem, smem, smem],
        out_specs=[vmem, vmem],
        scratch_shapes=[
            pltpu.VMEM((rows_s, weeks, cols), f32),
            pltpu.VMEM((rows_s, weeks, cols), f32),
            pltpu.VMEM((rows_s, padded, cols), f32),
            pltpu.VMEM((rows_s, padded, cols), f32),
            pltpu.VMEM((crews, cols), jnp.bfloat16),
            pltpu.VMEM((half, 128), f32),
            pltpu.VMEM((128, half), f32),
            pltpu.VMEM((rows_s, padded, cols), f32),
            pltpu.VMEM((rows_s, max(rows for _, rows in GROUPS) + 8, cols), f32),
            *each(2, rows_s, "r", half),
            *each(ITERS, rows_s, "r", half),
            *each(ITERS, 2, 5, "r", half),
            *each(ITERS, "r", half),
            *each(5, "r", half),
            *each(ITERS, 4, "r", half),
            *each(ITERS, 2, rows_s, "r", half),
            *each(2, "e", cols),
            *each(4, "e", cols),
            pltpu.SemaphoreType.DMA((2,)),
            pltpu.SemaphoreType.DMA((copies,)),
            pltpu.SemaphoreType.DMA((copies,)),
            pltpu.SemaphoreType.DMA((4 * len(GROUPS),)),
            pltpu.SemaphoreType.DMA((4 * len(GROUPS),)),
        ],
        compiler_params=pltpu.CompilerParams(
            collective_id=0, has_side_effects=True, vmem_limit_bytes=48 << 20
        ),
        name="hedge",
    )(
        multiplier, consensus_old, failure_week, crew_index.reshape(1, -1),
        labor_hours.reshape(1, -1), capacity, risk_weight.reshape(1, -1), likelihood, bundle_index,
    )


def solution(mesh):
    return jax.shard_map(
        local,
        mesh=mesh,
        in_specs=(
            P("scen", None, "comp"),
            P(None, None, "comp"),
            P("scen", "comp"),
            P("comp"),
            P("comp"),
            P(),
            P("comp"),
            P("scen"),
            P("scen"),
        ),
        out_specs=(P("scen", None, "comp"), P("scen", None, "comp")),
        check_vma=False,
    )
```

```python
import jax
import jax.numpy as jnp
from jax import lax
from jax.experimental import pallas as pl
from jax.experimental.pallas import tpu as pltpu
from jax.sharding import PartitionSpec as P

MESH = pl.DeviceIdType.MESH
ITERS = 3
STEP = 0.18
CREW_WEIGHT = 1.0
PLACES = (6, -6, 3, -3, 0, 7, -5, 4, -2, 1, 5, -7, 2, -4, -1, 8)
TILES = (2, 2, 2, 1)
ORDER = (
    0, 1, 2, 3, 0, 1, 2, 3, 0, 1, 2, 3, 0, 1, 2, 3, 0, 1, 2, 3,
    0, 1, 0, 2, 1, 3, 0, 2, 1, 3, 2, 3, 0, 1, 2, 3, 0, 1, 2, 3,
    0, 1, 2, 3, 0, 1, 0, 2, 1, 3, 0, 2, 1, 3, 2, 3, 0, 1, 2, 3,
    0, 1, 2, 3, 0, 1, 2, 3, 0, 1, 0, 2, 1, 3, 2, 3,
)
NCOPY = 17
F32, BF16 = jnp.float32, jnp.bfloat16


def split(x):
    high = x.astype(BF16)
    low = (x - high.astype(F32)).astype(BF16)
    return high, low


def dot(a, b):
    return jnp.dot(a, b, preferred_element_type=F32)


def kernel(
    mult_hbm, cons_hbm, fw_hbm, crew_hbm, labor_hbm, cap_hbm, risk_hbm, like_hbm, bundle_hbm,
    new_ref, bc_ref,
    fw_ref, crew_ref, labor_ref, cap_ref, risk_ref, like_ref, bundle_ref,
    mult, cons, plan, base, hot, cap_rows, mixer, likes, means,
    load_sem, store_sem, send_sem, recv_sem,
    edge_send, edge_recv, *per_group,
):
    groups = range(len(TILES))
    parts, cores, nears, opps, hubs, fars, excs, edges, gots = (
        per_group[n:n + len(TILES)] for n in range(0, len(per_group), len(TILES))
    )
    scen_count = lax.axis_size("scen")
    comp_count = lax.axis_size("comp")
    chips = comp_count // 2
    me_s = lax.axis_index("scen")
    me_c = lax.axis_index("comp")
    z = me_c // 2
    k = lax.rem(me_c, 2)
    weeks = cap_ref.shape[0]
    live, cols = mult_hbm.shape
    scens = live // weeks
    crews = hot.shape[0]
    half = crews // 2
    rows_of = [8 * n for n in TILES]
    first_of = [chips * sum(rows_of[:g]) for g in groups]

    def chip(step):
        return (me_s, lax.rem(z + step + chips, chips) * 2 + k)

    def row(step):
        return (lax.rem(me_s + step + scen_count, scen_count), me_c)

    def block(g, step):
        d = lax.rem(z + step + chips, chips)
        return pl.ds(pl.multiple_of(first_of[g] + d * rows_of[g], 8), rows_of[g])

    other = (me_s, z * 2 + 1 - k)

    loads = [
        pltpu.make_async_copy(source, target, load_sem.at[n])
        for n, (source, target) in enumerate((
            (crew_hbm, crew_ref), (bundle_hbm, bundle_ref), (labor_hbm, labor_ref),
            (cons_hbm, cons), (risk_hbm, risk_ref), (cap_hbm, cap_ref), (like_hbm, like_ref),
            (fw_hbm, fw_ref), (mult_hbm, mult),
        ))
    ]
    for load in loads:
        load.start()

    barrier = pltpu.get_barrier_semaphore()
    greeted = [other] + [chip(n) for n in (1, -1, 2, -2, 3, -3, 6, -6)] + [row(n) for n in (1, -1, 2, -2)]
    for device in greeted:
        pl.semaphore_signal(barrier, inc=1, device_id=device, device_id_type=MESH)

    padded = plan.shape[0]
    plan[live:, :] = jnp.zeros((padded - live, cols), F32)
    base[live:, :] = jnp.zeros((padded - live, cols), F32)
    cap_rows[live:, :] = jnp.zeros((padded - live, half), F32)
    loads[0].wait()
    hot[...] = (
        lax.broadcasted_iota(jnp.int32, (crews, cols), 0) == crew_ref[...]
    ).astype(BF16)
    coupling = CREW_WEIGHT * crews / (cols * comp_count)

    def by_scenario(ref, scenario):
        out = jnp.full(scenario.shape, ref[0])
        for s in range(1, scens):
            out = jnp.where(scenario == s, ref[s], out)
        return out

    loads[1].wait()
    span = 256
    r = lax.broadcasted_iota(jnp.int32, (span, span), 0)
    c = lax.broadcasted_iota(jnp.int32, (span, span), 1)
    want = by_scenario(bundle_ref, lax.rem(lax.broadcasted_iota(jnp.int32, (span, 128), 0), scens))
    want = jnp.concatenate([want] * (span // 128), axis=1)
    mixer[...] = (want + (r // scens) * scens == c).astype(BF16)
    loads[3].wait()
    loads[2].wait()
    labor = labor_ref[...]
    for at in range(0, live, span):
        size = min(span, live - at)
        x = cons[at:at + size, :]
        high, low = split(x)
        lower = (x - high.astype(F32) - low.astype(F32)).astype(BF16)
        take = mixer[:size, :size]
        plan[at:at + size, :] = dot(take, high) + dot(take, low) + dot(take, lower)

    flying = {}

    def start(g, t, n, source, target, device):
        at = (g * ITERS + t) * NCOPY + n
        flying[g, t, n] = pltpu.make_async_remote_copy(
            src_ref=source, dst_ref=target, send_sem=send_sem.at[at], recv_sem=recv_sem.at[at],
            device_id=device, device_id_type=MESH,
        )
        flying[g, t, n].start()

    def sent(g, t, numbers):
        for n in numbers:
            flying.pop((g, t, n)).wait_send()

    def arrive(g, t, numbers):
        for n in numbers:
            flying[g, t, n].wait_recv()

    def update(g, t):
        rows = rows_of[g]
        many = chips if TILES[g] == 1 else 8 if TILES[g] == 2 else 4
        for place in range(0, chips, many):
            blocks = [block(g, PLACES[place + n]) for n in range(many)]
            old = jnp.concatenate([plan[b, :] for b in blocks], axis=0)
            if t >= 0:
                fixed = jnp.concatenate([base[b, :] for b in blocks], axis=0)
                pushed = 0.0
                for h in range(2):
                    high, low = split(
                        excs[g][t, h, place:place + many].reshape(many * rows, half)
                    )
                    way = hot[h * half:(h + 1) * half, :]
                    pushed = pushed + dot(high, way) + dot(low, way)
                alpha = 1.0 - STEP * (risk_ref[...] + 1.0)
                beta = (STEP * coupling) * labor
                old = jnp.clip(alpha * old + fixed - beta * pushed, 0.0, 1.0)
                for n, b in enumerate(blocks):
                    plan[b, :] = old[n * rows:(n + 1) * rows]
            if t < ITERS - 1:
                high, low = split(old * labor)
                dims = (((1,), (1,)), ((), ()))
                out = lax.dot_general(high, hot[...], dims, preferred_element_type=F32)
                out = out + lax.dot_general(low, hot[...], dims, preferred_element_type=F32)
                for h in range(2):
                    parts[g][h, place:place + many] = out[:, h * half:(h + 1) * half].reshape(
                        many, rows, half
                    )

    def phase_core(g, t):
        if t > 0:
            arrive(g, t - 1, (15, 16))
            sent(g, t - 1, (0,))
        update(g, t - 1)
        if t == 0 and g == 0:
            pl.semaphore_wait(barrier, len(greeted))
        start(g, t, 0, parts[g].at[1 - k], cores[g].at[t], other)

    def phase_near(g, t):
        arrive(g, t, (0,))
        cores[g][t] = cores[g][t] + parts[g][k]
        mine = cores[g].at[t]
        start(g, t, 1, mine.at[pl.ds(5, 5)], nears[g].at[t, 0], chip(1))
        start(g, t, 2, mine.at[pl.ds(10, 5)], nears[g].at[t, 1], chip(-1))
        start(g, t, 3, mine.at[15], opps[g].at[t], chip(4 * k - 2))

    def phase_far(g, t):
        if t > 0:
            sent(g, t - 1, (4, 5, 6, 7))
        arrive(g, t, (1, 2, 3))
        hubs[g][...] = cores[g][t, 0:5] + nears[g][t, 0] + nears[g][t, 1]
        hubs[g][1 - k] = hubs[g][1 - k] + opps[g][t]
        for n, step in enumerate((6, -6, 3, -3)):
            start(g, t, 4 + n, hubs[g].at[n], fars[g].at[t, n], chip(step))

    def phase_back(g, t):
        arrive(g, t, range(4, 8))
        far = fars[g][t]
        total = hubs[g][4] + (far[0] + far[1]) + (far[2] + far[3])
        excs[g][t, k, 4] = jnp.maximum(total - cap_rows[block(g, 0), :], 0.0)
        own = excs[g].at[t, k, 4]
        for n, step in enumerate((6, -6, 3, -3)):
            start(g, t, 8 + n, own, excs[g].at[t, k, n ^ 1], chip(step))

    def phase_spread(g, t):
        arrive(g, t, range(8, 12))
        mine = excs[g].at[t, k]
        start(g, t, 12, mine.at[pl.ds(0, 5)], mine.at[pl.ds(10, 5)], chip(1))
        start(g, t, 13, mine.at[pl.ds(0, 5)], mine.at[pl.ds(5, 5)], chip(-1))
        start(g, t, 14, mine.at[1 - k], mine.at[15], chip(2 - 4 * k))
        start(g, t, 15, mine.at[pl.ds(0, 5)], mine.at[pl.ds(0, 5)], other)

    def phase_share(g, t):
        arrive(g, t, (12, 13, 14))
        mine = excs[g].at[t, k]
        start(g, t, 16, mine.at[pl.ds(5, 11)], mine.at[pl.ds(5, 11)], other)

    def prepare():
        for load in loads[4:7]:
            load.wait()
        mine = cap_ref[:, pl.ds(pl.multiple_of(k * half, half), half)]
        for w in range(weeks):
            cap_rows[w * scens:(w + 1) * scens, :] = jnp.broadcast_to(
                mine[w:w + 1, :], (scens, half)
            )
        for load in loads[7:]:
            load.wait()
        risk = risk_ref[...]
        fail = fw_ref[...]
        for w in range(weeks):
            spacing = (fail - w).astype(F32)
            target = jnp.where(spacing >= 0, 1.0 / (1.0 + (spacing * 0.25) ** 2), 0.25)
            at = slice(w * scens, (w + 1) * scens)
            base[at, :] = STEP * (risk * target - mult[at, :] + plan[at, :])
        have = by_scenario(
            bundle_ref, lax.rem(lax.broadcasted_iota(jnp.int32, (span, 128), 1), scens)
        )
        have = jnp.concatenate([have] * (span // 128), axis=1)
        take = (want == have).astype(F32)
        mixer[...] = jnp.where(r // scens == c // scens, take, 0.0).astype(BF16)
        likes[...] = by_scenario(like_ref, lax.broadcasted_iota(jnp.int32, (scens, cols), 0))

    head, tail = bundle_ref[0], bundle_ref[scens - 1]
    moving = {}

    def edge_start(g, n, source, step):
        at = g * 4 + n
        moving[g, n] = pltpu.make_async_remote_copy(
            src_ref=source, dst_ref=gots[g].at[n], send_sem=edge_send.at[at],
            recv_sem=edge_recv.at[at], device_id=row(step), device_id_type=MESH,
        )
        moving[g, n].start()

    def weeks_of(g):
        lowest = first_of[g] // scens
        return lowest, min(weeks, lowest + chips * rows_of[g] // scens)

    def phase_edges(g, t):
        arrive(g, t - 1, (15, 16))
        update(g, t - 1)
        count = chips * rows_of[g]
        at = slice(first_of[g], first_of[g] + count)
        x = plan[at, :].reshape(count // scens, scens, cols) * likes[...][None]
        high, low = split(x.reshape(count, cols))
        for n, (which, step) in enumerate(((tail, 1), (head, -1))):
            kept = edges[g].shape[1] - (8 if g == 0 else 0)
            week = lax.broadcasted_iota(jnp.int32, (kept, count), 0)
            place = lax.broadcasted_iota(jnp.int32, (kept, count), 1)
            flag = by_scenario(bundle_ref, lax.rem(place, scens)) == which
            take = jnp.where(place // scens == week, flag.astype(F32), 0.0).astype(BF16)
            edges[g][n, 0:kept] = dot(take, high) + dot(take, low)
            if g == 0:
                weight = jnp.float32(0.0)
                for s in range(scens):
                    weight = weight + jnp.where(bundle_ref[s] == which, like_ref[s], 0.0)
                edges[g][n, kept:kept + 8] = jnp.where(
                    lax.broadcasted_iota(jnp.int32, (8, cols), 0) < 4,
                    which.astype(F32), weight,
                )
            edge_start(g, n, edges[g].at[n], step)
            edge_start(g, n + 2, edges[g].at[n], 2 * step)
        for low_row in range(0, count, span):
            size = min(span, count - low_row)
            take = mixer[:size, :size]
            means[first_of[g] + low_row:first_of[g] + low_row + size, :] = (
                dot(take, high[low_row:low_row + size]) + dot(take, low[low_row:low_row + size])
            )
    phases = (phase_core, phase_near, phase_far, phase_back, phase_spread, phase_share)
    steps = [iter([(p, t) for t in range(ITERS) for p in phases] + [(phase_edges, ITERS)])
             for _ in groups]
    for n, g in enumerate(ORDER):
        if n == 2 * len(TILES):
            prepare()
        phase, t = next(steps[g])
        phase(g, t)
    high, low = split(likes[...])
    take = mixer[:scens, :scens]
    weight = dot(take, high) + dot(take, low)
    own = by_scenario(bundle_ref, lax.broadcasted_iota(jnp.int32, (scens, cols), 0))
    at_head, at_tail = (own == head).astype(F32), (own == tail).astype(F32)
    flags, stores = {}, []
    for g in groups:
        lowest, highest = weeks_of(g)
        for n in range(4):
            moving[g, n].wait_recv()
        got = gots[g]
        if g == 0:
            kept = got.shape[1] - 8
            for n in range(4):
                which = tail if n % 2 else head
                flags[n] = (got[n, kept:kept + 1, :] == which.astype(F32)).astype(F32)
                more = flags[n] * got[n, kept + 4:kept + 5, :]
                weight = weight + (at_tail if n % 2 else at_head) * more
            weight = 1.0 / weight
        left = flags[0] * got[0] + flags[2] * got[2]
        right = flags[1] * got[1] + flags[3] * got[3]
        for w in range(lowest, highest):
            at = slice(w * scens, (w + 1) * scens)
            n = w - lowest
            mean = weight * (
                means[at, :] + at_head * left[n:n + 1, :] + at_tail * right[n:n + 1, :]
            )
            means[at, :] = mean
            mult[at, :] = mult[at, :] + (plan[at, :] - mean)
        at = pl.ds(lowest * scens, (highest - lowest) * scens)
        for n, (source, target) in enumerate(((mult, new_ref), (means, bc_ref))):
            stores.append(
                pltpu.make_async_copy(source.at[at], target.at[at], store_sem.at[2 * g + n])
            )
            stores[-1].start()
    for store in stores:
        store.wait()
    for c in (*flying.values(), *moving.values()):
        c.wait_send()


def deliver(a_ref, b_ref, a_out, b_out, room, taken, given):
    pieces = room.shape[1]
    size = room.shape[2]
    ins, outs = [], []
    for n in range(pieces):
        at = pl.ds(n * size, size)
        for m, (source, target) in enumerate(((a_ref, a_out), (b_ref, b_out))):
            ins.append(pltpu.make_async_copy(source.at[at], room.at[m, n], taken.at[m, n]))
            outs.append(pltpu.make_async_copy(room.at[m, n], target.at[at], given.at[m, n]))
    for copy in ins:
        copy.start()
    for copy, onward in zip(ins, outs, strict=True):
        copy.wait()
        onward.start()
    for copy in outs:
        copy.wait()


def local(
    multiplier, consensus_old, failure_week, crew_index, labor_hours, capacity, risk_weight,
    likelihood, bundle_index,
):
    scens, weeks, cols = multiplier.shape
    crews = capacity.shape[0]
    half = crews // 2
    chips = lax.axis_size("comp") // 2
    live = scens * weeks
    padded = chips * 8 * sum(TILES)

    def each(*shape):
        return [pltpu.VMEM(tuple(8 * n if s == "r" else s for s in shape), F32) for n in TILES]

    def edge(count):
        return [
            pltpu.VMEM((count, chips * 8 * n // scens + (8 if g == 0 else 0), cols), F32)
            for g, n in enumerate(TILES)
        ]

    def flat(x):
        return jnp.swapaxes(x, 0, 1).reshape(live, cols)

    hbm = pl.BlockSpec(memory_space=pltpu.HBM)
    copies = len(TILES) * ITERS * NCOPY
    outs = pl.pallas_call(
        kernel,
        out_shape=[jax.ShapeDtypeStruct((live, cols), F32)] * 2,
        in_specs=[hbm] * 9,
        out_specs=[hbm, hbm],
        scratch_shapes=[
            pltpu.VMEM((scens, cols), jnp.int32),
            pltpu.VMEM((1, cols), jnp.int32),
            pltpu.VMEM((1, cols), F32),
            pltpu.VMEM((weeks, crews), F32),
            pltpu.VMEM((1, cols), F32),
            pltpu.SMEM((scens,), F32),
            pltpu.SMEM((scens,), jnp.int32),
            pltpu.VMEM((live, cols), F32),
            pltpu.VMEM((live, cols), F32),
            pltpu.VMEM((padded, cols), F32),
            pltpu.VMEM((padded, cols), F32),
            pltpu.VMEM((crews, cols), BF16),
            pltpu.VMEM((padded, half), F32),
            pltpu.VMEM((256, 256), BF16),
            pltpu.VMEM((scens, cols), F32),
            pltpu.VMEM((padded, cols), F32),
            pltpu.SemaphoreType.DMA((9,)),
            pltpu.SemaphoreType.DMA((2 * len(TILES),)),
            pltpu.SemaphoreType.DMA((copies,)),
            pltpu.SemaphoreType.DMA((copies,)),
            pltpu.SemaphoreType.DMA((4 * len(TILES),)),
            pltpu.SemaphoreType.DMA((4 * len(TILES),)),
            *each(2, chips, "r", half),
            *each(ITERS, chips, "r", half),
            *each(ITERS, 2, 5, "r", half),
            *each(ITERS, "r", half),
            *each(5, "r", half),
            *each(ITERS, 4, "r", half),
            *each(ITERS, 2, chips, "r", half),
            *edge(2),
            *edge(4),
        ],
        compiler_params=pltpu.CompilerParams(
            collective_id=0, has_side_effects=True, vmem_limit_bytes=60 << 20
        ),
        name="hedge",
    )(
        flat(multiplier), flat(consensus_old), failure_week, crew_index.reshape(1, -1),
        labor_hours.reshape(1, -1), capacity.T, risk_weight.reshape(1, -1), likelihood, bundle_index,
    )
    pieces = 4
    outs = pl.pallas_call(
        deliver,
        out_shape=[jax.ShapeDtypeStruct((live, cols), F32)] * 2,
        in_specs=[hbm] * 2,
        out_specs=[hbm] * 2,
        scratch_shapes=[
            pltpu.VMEM((2, pieces, live // pieces, cols), F32),
            pltpu.SemaphoreType.DMA((2, pieces)),
            pltpu.SemaphoreType.DMA((2, pieces)),
        ],
        compiler_params=pltpu.CompilerParams(vmem_limit_bytes=60 << 20),
        name="deliver",
    )(*outs)
    return tuple(jnp.swapaxes(x.reshape(weeks, scens, cols), 0, 1) for x in outs)


def solution(mesh):
    return jax.shard_map(
        local,
        mesh=mesh,
        in_specs=(
            P("scen", None, "comp"),
            P(None, None, "comp"),
            P("scen", "comp"),
            P("comp"),
            P("comp"),
            P(),
            P("comp"),
            P("scen"),
            P("scen"),
        ),
        out_specs=(P("scen", None, "comp"), P("scen", None, "comp")),
        check_vma=False,
    )
```

```python
import jax
import jax.numpy as jnp
from jax import lax
from jax.experimental import pallas as pl
from jax.experimental.pallas import tpu as pltpu
from jax.sharding import PartitionSpec as P

MESH = pl.DeviceIdType.MESH
ITERS = 3
STEP = 0.18
CREW_WEIGHT = 1.0
PLACES = (6, -6, 3, -3, 0, 7, -5, 4, -2, 1, 5, -7, 2, -4, -1, 8)
TILES = (2, 2, 2, 1)
ORDER = (
    0, 1, 2, 3, 0, 1, 2, 3, 0, 1, 2, 3, 0, 1, 2, 3, 0, 1, 2, 3,
    0, 1, 0, 2, 1, 3, 0, 2, 1, 3, 2, 3, 0, 1, 2, 3, 0, 1, 2, 3,
    0, 1, 2, 3, 0, 1, 0, 2, 1, 3, 0, 2, 1, 3, 2, 3, 0, 1, 2, 3,
    0, 1, 2, 3, 0, 1, 2, 3, 0, 1, 0, 2, 1, 3, 2, 3,
)
NCOPY = 17
F32, BF16 = jnp.float32, jnp.bfloat16


def split(x):
    high = x.astype(BF16)
    low = (x - high.astype(F32)).astype(BF16)
    return high, low


def dot(a, b):
    return jnp.dot(a, b, preferred_element_type=F32)


def kernel(
    mult_hbm, cons_hbm, fw_hbm, crew_hbm, labor_hbm, cap_hbm, risk_hbm, like_hbm, bundle_hbm,
    new_ref, bc_ref,
    fw_ref, crew_ref, labor_ref, cap_ref, risk_ref, like_ref, bundle_ref,
    mult, cons, plan, base, hot, cap_rows, mixer, likes, means,
    load_sem, store_sem, send_sem, recv_sem,
    edge_send, edge_recv, *per_group,
):
    groups = range(len(TILES))
    parts, cores, nears, opps, hubs, fars, excs, edges, gots = (
        per_group[n:n + len(TILES)] for n in range(0, len(per_group), len(TILES))
    )
    scen_count = lax.axis_size("scen")
    comp_count = lax.axis_size("comp")
    chips = comp_count // 2
    me_s = lax.axis_index("scen")
    me_c = lax.axis_index("comp")
    z = me_c // 2
    k = lax.rem(me_c, 2)
    weeks = cap_ref.shape[0]
    live, cols = mult_hbm.shape
    scens = live // weeks
    crews = hot.shape[0]
    half = crews // 2
    rows_of = [8 * n for n in TILES]
    first_of = [chips * sum(rows_of[:g]) for g in groups]

    def chip(step):
        return (me_s, lax.rem(z + step + chips, chips) * 2 + k)

    def row(step):
        return (lax.rem(me_s + step + scen_count, scen_count), me_c)

    def block(g, step):
        d = lax.rem(z + step + chips, chips)
        return pl.ds(pl.multiple_of(first_of[g] + d * rows_of[g], 8), rows_of[g])

    other = (me_s, z * 2 + 1 - k)

    loads = [
        pltpu.make_async_copy(source, target, load_sem.at[n])
        for n, (source, target) in enumerate((
            (crew_hbm, crew_ref), (bundle_hbm, bundle_ref), (labor_hbm, labor_ref),
            (cons_hbm, cons), (risk_hbm, risk_ref), (cap_hbm, cap_ref), (like_hbm, like_ref),
            (fw_hbm, fw_ref), (mult_hbm, mult),
        ))
    ]
    for load in loads[:4]:
        load.start()

    barrier = pltpu.get_barrier_semaphore()
    greeted = [other] + [chip(n) for n in (1, -1, 2, -2, 3, -3, 6, -6)] + [row(n) for n in (1, -1, 2, -2)]
    for device in greeted:
        pl.semaphore_signal(barrier, inc=1, device_id=device, device_id_type=MESH)

    padded = plan.shape[0]
    plan[live:, :] = jnp.zeros((padded - live, cols), F32)
    base[live:, :] = jnp.zeros((padded - live, cols), F32)
    cap_rows[live:, :] = jnp.zeros((padded - live, half), F32)
    loads[0].wait()
    hot[...] = (
        lax.broadcasted_iota(jnp.int32, (crews, cols), 0) == crew_ref[...]
    ).astype(BF16)
    coupling = CREW_WEIGHT * crews / (cols * comp_count)

    def by_scenario(ref, scenario):
        out = jnp.full(scenario.shape, ref[0])
        for s in range(1, scens):
            out = jnp.where(scenario == s, ref[s], out)
        return out

    loads[1].wait()
    span = 256
    r = lax.broadcasted_iota(jnp.int32, (span, span), 0)
    c = lax.broadcasted_iota(jnp.int32, (span, span), 1)
    want = by_scenario(bundle_ref, lax.rem(lax.broadcasted_iota(jnp.int32, (span, 128), 0), scens))
    want = jnp.concatenate([want] * (span // 128), axis=1)
    mixer[...] = (want + (r // scens) * scens == c).astype(BF16)
    loads[3].wait()
    loads[2].wait()
    labor = labor_ref[...]
    for load in loads[4:]:
        load.start()

    def anchor(g):
        last = min(live, first_of[g] + chips * rows_of[g])
        for at in range(first_of[g], last, span):
            size = min(span, last - at)
            x = cons[at:at + size, :]
            high, low = split(x)
            lower = (x - high.astype(F32) - low.astype(F32)).astype(BF16)
            take = mixer[:size, :size]
            plan[at:at + size, :] = dot(take, high) + dot(take, low) + dot(take, lower)

    flying = {}

    def start(g, t, n, source, target, device):
        at = (g * ITERS + t) * NCOPY + n
        flying[g, t, n] = pltpu.make_async_remote_copy(
            src_ref=source, dst_ref=target, send_sem=send_sem.at[at], recv_sem=recv_sem.at[at],
            device_id=device, device_id_type=MESH,
        )
        flying[g, t, n].start()

    def sent(g, t, numbers):
        for n in numbers:
            flying.pop((g, t, n)).wait_send()

    def arrive(g, t, numbers):
        for n in numbers:
            flying[g, t, n].wait_recv()

    def update(g, t):
        rows = rows_of[g]
        many = chips if TILES[g] == 1 else 8 if TILES[g] == 2 else 4
        for place in range(0, chips, many):
            blocks = [block(g, PLACES[place + n]) for n in range(many)]
            old = jnp.concatenate([plan[b, :] for b in blocks], axis=0)
            if t >= 0:
                fixed = jnp.concatenate([base[b, :] for b in blocks], axis=0)
                pushed = 0.0
                for h in range(2):
                    high, low = split(
                        excs[g][t, h, place:place + many].reshape(many * rows, half)
                    )
                    way = hot[h * half:(h + 1) * half, :]
                    pushed = pushed + dot(high, way) + dot(low, way)
                alpha = 1.0 - STEP * (risk_ref[...] + 1.0)
                beta = (STEP * coupling) * labor
                old = jnp.clip(alpha * old + fixed - beta * pushed, 0.0, 1.0)
                for n, b in enumerate(blocks):
                    plan[b, :] = old[n * rows:(n + 1) * rows]
            if t < ITERS - 1:
                high, low = split(old * labor)
                dims = (((1,), (1,)), ((), ()))
                out = lax.dot_general(high, hot[...], dims, preferred_element_type=F32)
                out = out + lax.dot_general(low, hot[...], dims, preferred_element_type=F32)
                for h in range(2):
                    parts[g][h, place:place + many] = out[:, h * half:(h + 1) * half].reshape(
                        many, rows, half
                    )

    def phase_core(g, t):
        if t > 0:
            arrive(g, t - 1, (15, 16))
            sent(g, t - 1, (0,))
        else:
            anchor(g)
        update(g, t - 1)
        if t == 0 and g == 0:
            pl.semaphore_wait(barrier, len(greeted))
        start(g, t, 0, parts[g].at[1 - k], cores[g].at[t], other)

    def phase_near(g, t):
        arrive(g, t, (0,))
        cores[g][t] = cores[g][t] + parts[g][k]
        mine = cores[g].at[t]
        start(g, t, 1, mine.at[pl.ds(5, 5)], nears[g].at[t, 0], chip(1))
        start(g, t, 2, mine.at[pl.ds(10, 5)], nears[g].at[t, 1], chip(-1))
        start(g, t, 3, mine.at[15], opps[g].at[t], chip(4 * k - 2))

    def phase_far(g, t):
        if t > 0:
            sent(g, t - 1, (4, 5, 6, 7))
        arrive(g, t, (1, 2, 3))
        hubs[g][...] = cores[g][t, 0:5] + nears[g][t, 0] + nears[g][t, 1]
        hubs[g][1 - k] = hubs[g][1 - k] + opps[g][t]
        for n, step in enumerate((6, -6, 3, -3)):
            start(g, t, 4 + n, hubs[g].at[n], fars[g].at[t, n], chip(step))

    def phase_back(g, t):
        arrive(g, t, range(4, 8))
        far = fars[g][t]
        total = hubs[g][4] + (far[0] + far[1]) + (far[2] + far[3])
        excs[g][t, k, 4] = jnp.maximum(total - cap_rows[block(g, 0), :], 0.0)
        own = excs[g].at[t, k, 4]
        for n, step in enumerate((6, -6, 3, -3)):
            start(g, t, 8 + n, own, excs[g].at[t, k, n ^ 1], chip(step))

    def phase_spread(g, t):
        arrive(g, t, range(8, 12))
        mine = excs[g].at[t, k]
        start(g, t, 12, mine.at[pl.ds(0, 5)], mine.at[pl.ds(10, 5)], chip(1))
        start(g, t, 13, mine.at[pl.ds(0, 5)], mine.at[pl.ds(5, 5)], chip(-1))
        start(g, t, 14, mine.at[1 - k], mine.at[15], chip(2 - 4 * k))
        start(g, t, 15, mine.at[pl.ds(0, 5)], mine.at[pl.ds(0, 5)], other)

    def phase_share(g, t):
        arrive(g, t, (12, 13, 14))
        mine = excs[g].at[t, k]
        start(g, t, 16, mine.at[pl.ds(5, 11)], mine.at[pl.ds(5, 11)], other)

    def prepare():
        for load in loads[4:7]:
            load.wait()
        mine = cap_ref[:, pl.ds(pl.multiple_of(k * half, half), half)]
        for w in range(weeks):
            cap_rows[w * scens:(w + 1) * scens, :] = jnp.broadcast_to(
                mine[w:w + 1, :], (scens, half)
            )
        for load in loads[7:]:
            load.wait()
        risk = risk_ref[...]
        fail = fw_ref[...]
        for w in range(weeks):
            spacing = (fail - w).astype(F32)
            target = jnp.where(spacing >= 0, 1.0 / (1.0 + (spacing * 0.25) ** 2), 0.25)
            at = slice(w * scens, (w + 1) * scens)
            base[at, :] = STEP * (risk * target - mult[at, :] + plan[at, :])
        have = by_scenario(
            bundle_ref, lax.rem(lax.broadcasted_iota(jnp.int32, (span, 128), 1), scens)
        )
        have = jnp.concatenate([have] * (span // 128), axis=1)
        take = (want == have).astype(F32)
        mixer[...] = jnp.where(r // scens == c // scens, take, 0.0).astype(BF16)
        likes[...] = by_scenario(like_ref, lax.broadcasted_iota(jnp.int32, (scens, cols), 0))

    head, tail = bundle_ref[0], bundle_ref[scens - 1]
    moving = {}

    def edge_start(g, n, source, step):
        at = g * 4 + n
        moving[g, n] = pltpu.make_async_remote_copy(
            src_ref=source, dst_ref=gots[g].at[n], send_sem=edge_send.at[at],
            recv_sem=edge_recv.at[at], device_id=row(step), device_id_type=MESH,
        )
        moving[g, n].start()

    def weeks_of(g):
        lowest = first_of[g] // scens
        return lowest, min(weeks, lowest + chips * rows_of[g] // scens)

    def phase_edges(g, t):
        arrive(g, t - 1, (15, 16))
        update(g, t - 1)
        count = chips * rows_of[g]
        at = slice(first_of[g], first_of[g] + count)
        x = plan[at, :].reshape(count // scens, scens, cols) * likes[...][None]
        high, low = split(x.reshape(count, cols))
        for n, (which, step) in enumerate(((tail, 1), (head, -1))):
            kept = edges[g].shape[1] - (8 if g == 0 else 0)
            week = lax.broadcasted_iota(jnp.int32, (kept, count), 0)
            place = lax.broadcasted_iota(jnp.int32, (kept, count), 1)
            flag = by_scenario(bundle_ref, lax.rem(place, scens)) == which
            take = jnp.where(place // scens == week, flag.astype(F32), 0.0).astype(BF16)
            edges[g][n, 0:kept] = dot(take, high) + dot(take, low)
            if g == 0:
                weight = jnp.float32(0.0)
                for s in range(scens):
                    weight = weight + jnp.where(bundle_ref[s] == which, like_ref[s], 0.0)
                edges[g][n, kept:kept + 8] = jnp.where(
                    lax.broadcasted_iota(jnp.int32, (8, cols), 0) < 4,
                    which.astype(F32), weight,
                )
            edge_start(g, n, edges[g].at[n], step)
            edge_start(g, n + 2, edges[g].at[n], 2 * step)
        for low_row in range(0, count, span):
            size = min(span, count - low_row)
            take = mixer[:size, :size]
            means[first_of[g] + low_row:first_of[g] + low_row + size, :] = (
                dot(take, high[low_row:low_row + size]) + dot(take, low[low_row:low_row + size])
            )
    phases = (phase_core, phase_near, phase_far, phase_back, phase_spread, phase_share)
    steps = [iter([(p, t) for t in range(ITERS) for p in phases] + [(phase_edges, ITERS)])
             for _ in groups]
    for n, g in enumerate(ORDER):
        if n == 2 * len(TILES):
            prepare()
        phase, t = next(steps[g])
        phase(g, t)
    high, low = split(likes[...])
    take = mixer[:scens, :scens]
    weight = dot(take, high) + dot(take, low)
    own = by_scenario(bundle_ref, lax.broadcasted_iota(jnp.int32, (scens, cols), 0))
    at_head, at_tail = (own == head).astype(F32), (own == tail).astype(F32)
    flags, stores = {}, []
    for g in groups:
        lowest, highest = weeks_of(g)
        for n in range(4):
            moving[g, n].wait_recv()
        got = gots[g]
        if g == 0:
            kept = got.shape[1] - 8
            for n in range(4):
                which = tail if n % 2 else head
                flags[n] = (got[n, kept:kept + 1, :] == which.astype(F32)).astype(F32)
                more = flags[n] * got[n, kept + 4:kept + 5, :]
                weight = weight + (at_tail if n % 2 else at_head) * more
            weight = 1.0 / weight
        left = flags[0] * got[0] + flags[2] * got[2]
        right = flags[1] * got[1] + flags[3] * got[3]
        for w in range(lowest, highest):
            at = slice(w * scens, (w + 1) * scens)
            n = w - lowest
            mean = weight * (
                means[at, :] + at_head * left[n:n + 1, :] + at_tail * right[n:n + 1, :]
            )
            means[at, :] = mean
            mult[at, :] = mult[at, :] + (plan[at, :] - mean)
        at = pl.ds(lowest * scens, (highest - lowest) * scens)
        for n, (source, target) in enumerate(((mult, new_ref), (means, bc_ref))):
            stores.append(
                pltpu.make_async_copy(source.at[at], target.at[at], store_sem.at[2 * g + n])
            )
            stores[-1].start()
    for store in stores:
        store.wait()
    for c in (*flying.values(), *moving.values()):
        c.wait_send()


def deliver(a_ref, b_ref, a_out, b_out, room, taken, given):
    pieces = room.shape[1]
    size = room.shape[2]
    ins, outs = [], []
    for n in range(pieces):
        at = pl.ds(n * size, size)
        for m, (source, target) in enumerate(((a_ref, a_out), (b_ref, b_out))):
            ins.append(pltpu.make_async_copy(source.at[at], room.at[m, n], taken.at[m, n]))
            outs.append(pltpu.make_async_copy(room.at[m, n], target.at[at], given.at[m, n]))
    for copy in ins:
        copy.start()
    for copy, onward in zip(ins, outs, strict=True):
        copy.wait()
        onward.start()
    for copy in outs:
        copy.wait()


def local(
    multiplier, consensus_old, failure_week, crew_index, labor_hours, capacity, risk_weight,
    likelihood, bundle_index,
):
    scens, weeks, cols = multiplier.shape
    crews = capacity.shape[0]
    half = crews // 2
    chips = lax.axis_size("comp") // 2
    live = scens * weeks
    padded = chips * 8 * sum(TILES)

    def each(*shape):
        return [pltpu.VMEM(tuple(8 * n if s == "r" else s for s in shape), F32) for n in TILES]

    def edge(count):
        return [
            pltpu.VMEM((count, chips * 8 * n // scens + (8 if g == 0 else 0), cols), F32)
            for g, n in enumerate(TILES)
        ]

    def flat(x):
        return jnp.swapaxes(x, 0, 1).reshape(live, cols)

    hbm = pl.BlockSpec(memory_space=pltpu.HBM)
    copies = len(TILES) * ITERS * NCOPY
    outs = pl.pallas_call(
        kernel,
        out_shape=[jax.ShapeDtypeStruct((live, cols), F32)] * 2,
        in_specs=[hbm] * 9,
        out_specs=[hbm, hbm],
        scratch_shapes=[
            pltpu.VMEM((scens, cols), jnp.int32),
            pltpu.VMEM((1, cols), jnp.int32),
            pltpu.VMEM((1, cols), F32),
            pltpu.VMEM((weeks, crews), F32),
            pltpu.VMEM((1, cols), F32),
            pltpu.SMEM((scens,), F32),
            pltpu.SMEM((scens,), jnp.int32),
            pltpu.VMEM((live, cols), F32),
            pltpu.VMEM((live, cols), F32),
            pltpu.VMEM((padded, cols), F32),
            pltpu.VMEM((padded, cols), F32),
            pltpu.VMEM((crews, cols), BF16),
            pltpu.VMEM((padded, half), F32),
            pltpu.VMEM((256, 256), BF16),
            pltpu.VMEM((scens, cols), F32),
            pltpu.VMEM((padded, cols), F32),
            pltpu.SemaphoreType.DMA((9,)),
            pltpu.SemaphoreType.DMA((2 * len(TILES),)),
            pltpu.SemaphoreType.DMA((copies,)),
            pltpu.SemaphoreType.DMA((copies,)),
            pltpu.SemaphoreType.DMA((4 * len(TILES),)),
            pltpu.SemaphoreType.DMA((4 * len(TILES),)),
            *each(2, chips, "r", half),
            *each(ITERS, chips, "r", half),
            *each(ITERS, 2, 5, "r", half),
            *each(ITERS, "r", half),
            *each(5, "r", half),
            *each(ITERS, 4, "r", half),
            *each(ITERS, 2, chips, "r", half),
            *edge(2),
            *edge(4),
        ],
        compiler_params=pltpu.CompilerParams(
            collective_id=0, has_side_effects=True, vmem_limit_bytes=60 << 20
        ),
        name="hedge",
    )(
        flat(multiplier), flat(consensus_old), failure_week, crew_index.reshape(1, -1),
        labor_hours.reshape(1, -1), capacity.T, risk_weight.reshape(1, -1), likelihood, bundle_index,
    )
    pieces = 4
    outs = pl.pallas_call(
        deliver,
        out_shape=[jax.ShapeDtypeStruct((live, cols), F32)] * 2,
        in_specs=[hbm] * 2,
        out_specs=[hbm] * 2,
        scratch_shapes=[
            pltpu.VMEM((2, pieces, live // pieces, cols), F32),
            pltpu.SemaphoreType.DMA((2, pieces)),
            pltpu.SemaphoreType.DMA((2, pieces)),
        ],
        compiler_params=pltpu.CompilerParams(vmem_limit_bytes=60 << 20),
        name="deliver",
    )(*outs)
    return tuple(jnp.swapaxes(x.reshape(weeks, scens, cols), 0, 1) for x in outs)


def solution(mesh):
    return jax.shard_map(
        local,
        mesh=mesh,
        in_specs=(
            P("scen", None, "comp"),
            P(None, None, "comp"),
            P("scen", "comp"),
            P("comp"),
            P("comp"),
            P(),
            P("comp"),
            P("scen"),
            P("scen"),
        ),
        out_specs=(P("scen", None, "comp"), P("scen", None, "comp")),
        check_vma=False,
    )
```
